256 devices in a mesh: dp: 4 (over y), row: 4 (over z_lo, core), col: 16 (over x, z_hi).
Axes of the slice: x: 4, y: 4, z: 8 (z_hi: 4, z_lo: 2; z = z_hi * 2 + z_lo), core: 2. Of those that a mesh axis runs over, the one named last changes fastest.
Arguments:
- tokens: bfloat16 [4096, 12288], P(('dp', 'col'), 'row'), may hold values from -6 to 6
- w_tiles: bfloat16 [4, 192, 8, 128, 128], P('row', 'col'), may hold values from -0.1875 to 0.1875
- tile_rows: int32 [4, 192, 8], P('row', 'col'), may hold values from 0 to 23, as said below
- tile_count: int32 [4, 192], P('row', 'col'), may hold values from 2 to 8, as said below
- grad_hidden: bfloat16 [4096, 24576], P(('dp', 'row'), 'col'), may hold values from -6 to 6
Outputs:
- hidden: bfloat16 [4096, 24576], P(('dp', 'row'), 'col')
- grad_tokens: bfloat16 [4096, 12288], P(('dp', 'col'), 'row')
- grad_weights: bfloat16 [4, 192, 8, 128, 128], P('row', 'col')
The draws below stay inside these ranges and needn't reach their ends.
Inputs may be any that keep to these rules, and one draw needn't show every extreme that they name: `tile_rows`: within each row group and panel the 8 entries are distinct. `tile_count`: in every row group some panel has exactly 8 live slots.
All inputs are finite; a program needn't handle non-finite values.
Results may differ from the reference program's by a relative error of at most 0.02.
Values may be sent and summed in bfloat16 or wider, within the bound.
No kernel may reach another device: no remote copies, remote signals or barrier semaphores. Data moves between devices by JAX's collectives and lax.ppermute only.
A program may use at most 128 MiB of HBM per device.

```python
from functools import partial
import jax
import jax.numpy as jnp
from jax import lax

D = 12288
FF = 24576
BLK = 128
KMAX = 8
GROUPS = 4
RGROUP = 24
PANELS = 192
TOKENS = 1024
ALL_TOKENS = 4096
N_DP = 4
N_COL = 16


def draw_tile_rows(key, part):
    key = jax.random.fold_in(key, 11)
    scores = jax.random.randint(key, (GROUPS, PANELS, RGROUP), 0, 4096)
    scores = scores * RGROUP + jnp.arange(RGROUP).astype(jnp.int32)
    order = jnp.argsort(scores, axis=-1)
    return order[..., :KMAX].astype(jnp.int32)


def draw_tile_count(key, part):
    key = jax.random.fold_in(key, 12)
    first_key, second_key = jax.random.split(key)
    base_count = jax.random.randint(first_key, (GROUPS, PANELS), 2, KMAX + 1)
    full_panel = jax.random.randint(second_key, (GROUPS, 1), 0, PANELS)
    panel_ids = jnp.arange(PANELS).astype(jnp.int32)[None, :]
    return jnp.where(panel_ids == full_panel, KMAX, base_count).astype(jnp.int32)


def with_spikes(entries, stream_key, source, target, blocks, factor):
    owner, partner = [(jnp.arange(entries.shape[axis_at]) // (entries.shape[axis_at] // blocks)).reshape([-1 if axis == axis_at else 1 for axis in range(entries.ndim)]) for axis_at in (source, target)]
    chosen = jax.random.permutation(stream_key, blocks)[partner]
    strong = (owner == chosen) | (owner == (partner + blocks // 2) % blocks)
    return jnp.where(strong, factor * entries, entries)


def level_of(key, extent, pieces, least, largest):
    factor_of = 1.0
    for dim, blocks in pieces:
        heights = jax.random.uniform(jax.random.fold_in(jax.random.fold_in(key, 6), dim), (blocks,), jnp.float32, least / len(pieces), largest / len(pieces))
        factor_of = factor_of * jnp.repeat(jnp.exp(heights), extent[dim] // blocks).reshape((-1,) + (1,) * (len(extent) - 1 - dim))
    return factor_of


def normal_values(key, shape, width, most, shards=(), dtype=jnp.bfloat16):
    result = jax.random.normal(key, shape, jnp.float32) * width
    if len(shards) > 0:
        result = level_of(key, shape, shards, -0.22, 0.18) * result
    return jnp.clip(result, min=-most, max=most).astype(dtype)


def gaussian_with(rng, extent, width, bound, pieces, heavy, kind=jnp.bfloat16):
    result = width * jax.random.normal(rng, extent, jnp.float32)
    if pieces:
        result = result * level_of(rng, extent, pieces, -0.22, 0.18)
    return jnp.clip(with_spikes(result, jax.random.fold_in(rng, 3), *heavy), -bound, bound).astype(kind)


def setup_inputs(seed: int = 0) -> dict:
    streams_of = jax.random.split(jax.random.key(seed), 6)
    tokens = normal_values(streams_of[0], (ALL_TOKENS, D), 1.0, 6.0, ((0, 64), (1, 4)))
    w_tiles = normal_values(streams_of[1], (GROUPS, PANELS, KMAX, BLK, BLK), (KMAX * BLK) ** -0.5, 0.1875, ((0, 4), (1, 16)))
    tile_rows = draw_tile_rows(jax.random.fold_in(streams_of[5], 71), 0)
    tile_count = draw_tile_count(jax.random.fold_in(streams_of[5], 71), 0)
    grad_hidden = gaussian_with(streams_of[4], (ALL_TOKENS, FF), 1.0, 6.0, ((0, 16), (1, 16)), (1, 0, 16, 2.0))
    return {"tokens": tokens, "w_tiles": w_tiles, "tile_rows": tile_rows, "tile_count": tile_count, "grad_hidden": grad_hidden}


def settle(values):
    return lax.optimization_barrier(values.astype(jnp.bfloat16)).astype(jnp.float32)

def reference(tokens, w_tiles, tile_rows, tile_count, grad_hidden):
    highest = lax.Precision.HIGHEST
    slot_range = jnp.arange(KMAX).astype(jnp.int32)
    live_slot = (slot_range[None, None, :] < tile_count[:, :, None]).astype(jnp.float32)
    weights = w_tiles.astype(jnp.float32) * live_slot[..., None, None]
    all_count = tokens.shape[0]
    by_block = tokens.astype(jnp.float32).reshape(all_count, GROUPS, RGROUP, BLK)
    group_ids = jnp.arange(GROUPS).astype(jnp.int32)[:, None]
    panel_ids = jnp.arange(PANELS).astype(jnp.int32)

    def select(panel):
        return by_block[:, group_ids, tile_rows[:, panel, :], :]

    def forward_panel(panel):
        parts = jnp.einsum('ngkb,gkbc->ngc', select(panel), weights[:, panel], precision=highest)
        return lax.optimization_barrier(jnp.sum(settle(parts), axis=1))
    pre_act = lax.map(forward_panel, panel_ids)
    pre_act = jnp.transpose(pre_act, (1, 0, 2)).reshape(all_count, FF)
    gelu_fn = partial(jax.nn.gelu, approximate=True)
    hidden = gelu_fn(pre_act).astype(jnp.bfloat16)
    _, backward = jax.vjp(gelu_fn, pre_act)
    grad_pre = backward(grad_hidden.astype(jnp.float32))[0].astype(jnp.bfloat16)
    grad_panels = grad_pre.astype(jnp.float32).reshape(all_count, PANELS, BLK)
    onehot = (tile_rows[..., None] == jnp.arange(RGROUP).astype(jnp.int32)).astype(jnp.float32)
    per_col = PANELS // N_COL

    def input_panel(carry, panel):
        spread = jnp.einsum('nc,gkbc->ngkb', grad_panels[:, panel], weights[:, panel], precision=highest)
        return (carry + jnp.einsum('ngkb,gkr->ngrb', spread, onehot[:, panel], precision=highest), None)

    def input_group(total_sum, column):
        zero_sum = jnp.zeros((all_count, GROUPS, RGROUP, BLK), jnp.float32)
        group_sum, _ = lax.scan(input_panel, zero_sum, column * per_col + jnp.arange(per_col).astype(jnp.int32))
        return (total_sum + settle(group_sum), None)
    start_sum = jnp.zeros((all_count, GROUPS, RGROUP, BLK), jnp.float32)
    grad_total, _ = lax.scan(input_group, start_sum, jnp.arange(N_COL).astype(jnp.int32))
    grad_tokens = grad_total.reshape(all_count, D).astype(jnp.bfloat16)

    def weight_panel(panel):
        chosen = select(panel).reshape(N_DP, TOKENS, GROUPS, KMAX, BLK)
        grads = grad_panels[:, panel].reshape(N_DP, TOKENS, BLK)
        per_rep = jnp.einsum('dngkb,dnc->dgkbc', chosen, grads, precision=highest)
        per_rep = per_rep * live_slot[None, :, panel, :, None, None]
        return lax.optimization_barrier(jnp.sum(settle(per_rep), axis=0))
    grad_weights = lax.map(weight_panel, panel_ids)
    grad_weights = jnp.transpose(grad_weights, (1, 0, 2, 3, 4)).astype(jnp.bfloat16)
    return (hidden, grad_tokens, grad_weights)
```

```python
from functools import partial

import jax
import jax.numpy as jnp
from jax import lax
from jax.experimental import pallas as pl
from jax.experimental.pallas import tpu as pltpu
from jax.sharding import PartitionSpec as P

VMEM_LIMIT = 48 * 1024 * 1024


def lanes(start, size):
    return pl.ds(pl.multiple_of(start * size, size), size)


def forward_kernel(rows, count, x_ref, w_ref, o_ref):
    panel = pl.program_id(0)
    slots, tile, _ = w_ref.shape[1:]
    live = count[panel]
    weights = jnp.concatenate(
        [w_ref[0, k] * (live > k).astype(jnp.bfloat16) for k in range(slots)], axis=0
    )
    block = 256

    def body(i, carry):
        at = pl.ds(pl.multiple_of(i * block, block), block)
        chosen = [x_ref[at, lanes(rows[panel * slots + k], tile)] for k in range(slots)]
        total = jnp.dot(
            jnp.concatenate(chosen, axis=1), weights, preferred_element_type=jnp.float32
        )
        o_ref[at, :] = total.astype(jnp.bfloat16)
        return carry

    lax.fori_loop(0, x_ref.shape[0] // block, body, 0)


def forward(rows, count, x, w):
    panels, slots, tile, _ = w.shape
    tokens, width = x.shape
    return pl.pallas_call(
        forward_kernel,
        grid_spec=pltpu.PrefetchScalarGridSpec(
            num_scalar_prefetch=2,
            grid=(panels,),
            in_specs=[
                pl.BlockSpec((tokens, width), lambda p, *_: (0, 0)),
                pl.BlockSpec((1, slots, tile, tile), lambda p, *_: (p, 0, 0, 0)),
            ],
            out_specs=pl.BlockSpec((tokens, tile), lambda p, *_: (0, p)),
        ),
        out_shape=jax.ShapeDtypeStruct((tokens, panels * tile), jnp.bfloat16),
        compiler_params=pltpu.CompilerParams(vmem_limit_bytes=VMEM_LIMIT),
        cost_estimate=pl.CostEstimate(
            flops=2 * tokens * panels * slots * tile * tile,
            bytes_accessed=2 * (tokens * width + w.size + tokens * panels * tile),
            transcendentals=0,
        ),
        name="forward",
    )(rows, count, x, w)


def transpose_kernel(x_ref, o_ref):
    o_ref[...] = x_ref[...].T


def transposed(x):
    tokens, width = x.shape
    step = 256
    return pl.pallas_call(
        transpose_kernel,
        grid=(width // step,),
        in_specs=[pl.BlockSpec((tokens, step), lambda i: (0, i))],
        out_specs=pl.BlockSpec((step, tokens), lambda i: (i, 0)),
        out_shape=jax.ShapeDtypeStruct((width, tokens), jnp.bfloat16),
        compiler_params=pltpu.CompilerParams(vmem_limit_bytes=16 * 1024 * 1024),
        cost_estimate=pl.CostEstimate(
            flops=0, bytes_accessed=4 * x.size, transcendentals=0
        ),
        name="transposed",
    )(x)


def weight_kernel(rows, count, xt_ref, g_ref, o_ref):
    panel = pl.program_id(0)
    slots, tile, _ = o_ref.shape[1:]
    live = count[panel]
    half = slots // 2
    for part in range(2):
        first = part * half

        @pl.when(live > first)
        def _():
            chosen = [xt_ref[rows[panel * slots + first + k]] for k in range(half)]
            total = jnp.dot(
                jnp.concatenate(chosen, axis=0), g_ref[...], preferred_element_type=jnp.float32
            )
            for k in range(half):
                block = total[k * tile : (k + 1) * tile]
                o_ref[0, first + k] = jnp.where(live > first + k, block, 0.0).astype(jnp.bfloat16)

        @pl.when(live <= first)
        def _():
            o_ref[0, first : first + half] = jnp.zeros((half, tile, tile), jnp.bfloat16)


def weight_grad(rows, count, xt, g, slots, tile):
    blocks, _, tokens = xt.shape
    panels = g.shape[1] // tile
    return pl.pallas_call(
        weight_kernel,
        grid_spec=pltpu.PrefetchScalarGridSpec(
            num_scalar_prefetch=2,
            grid=(panels,),
            in_specs=[
                pl.BlockSpec((blocks, tile, tokens), lambda p, *_: (0, 0, 0)),
                pl.BlockSpec((tokens, tile), lambda p, *_: (0, p)),
            ],
            out_specs=pl.BlockSpec((1, slots, tile, tile), lambda p, *_: (p, 0, 0, 0)),
        ),
        out_shape=jax.ShapeDtypeStruct((panels, slots, tile, tile), jnp.bfloat16),
        compiler_params=pltpu.CompilerParams(vmem_limit_bytes=VMEM_LIMIT),
        cost_estimate=pl.CostEstimate(
            flops=2 * tokens * panels * slots * tile * tile,
            bytes_accessed=2 * (xt.size + g.size + panels * slots * tile * tile),
            transcendentals=0,
        ),
        name="weight_grad",
    )(rows, count, xt, g)


def input_kernel(rows, count, g_ref, w_ref, o_ref, hits, found, total):
    row = pl.program_id(0)
    panels, slots, tile, _ = w_ref.shape
    blocks = pl.num_programs(0)

    @pl.when(row == 0)
    def _():
        def clear(r, carry):
            found[r] = 0
            return carry

        lax.fori_loop(0, blocks, clear, 0)

        def place(p, carry):
            for k in range(slots):

                @pl.when(count[p] > k)
                def _():
                    r = rows[p * slots + k]
                    n = found[r]
                    hits[r * panels + n] = p * slots + k
                    found[r] = n + 1

            return carry

        lax.fori_loop(0, panels, place, 0)

    n = found[row]
    total[...] = jnp.zeros_like(total)

    def pair(i, carry):
        first = hits[row * panels + 2 * i]
        both = 2 * i + 1 < n
        second = jnp.where(both, hits[row * panels + jnp.minimum(2 * i + 1, panels - 1)], first)
        p0, k0 = lax.div(first, slots), lax.rem(first, slots)
        p1, k1 = lax.div(second, slots), lax.rem(second, slots)
        weights = jnp.concatenate([w_ref[p0, k0], w_ref[p1, k1] * both.astype(jnp.bfloat16)], axis=1)
        grads = jnp.concatenate([g_ref[:, lanes(p0, tile)], g_ref[:, lanes(p1, tile)]], axis=1)
        total[...] += lax.dot_general(
            grads, weights, (((1,), (1,)), ((), ())), preferred_element_type=jnp.float32
        )
        return carry

    lax.fori_loop(0, lax.div(n + 1, 2), pair, 0)
    o_ref[...] = total[...].astype(jnp.bfloat16)


def input_grad(rows, count, g, w, blocks):
    panels, slots, tile, _ = w.shape
    tokens = g.shape[0]
    return pl.pallas_call(
        input_kernel,
        grid_spec=pltpu.PrefetchScalarGridSpec(
            num_scalar_prefetch=2,
            grid=(blocks,),
            in_specs=[
                pl.BlockSpec(g.shape, lambda r, *_: (0, 0)),
                pl.BlockSpec(w.shape, lambda r, *_: (0, 0, 0, 0)),
            ],
            out_specs=pl.BlockSpec((tokens, tile), lambda r, *_: (0, r)),
            scratch_shapes=[
                pltpu.SMEM((blocks * panels,), jnp.int32),
                pltpu.SMEM((blocks,), jnp.int32),
                pltpu.VMEM((tokens, tile), jnp.float32),
            ],
        ),
        out_shape=jax.ShapeDtypeStruct((tokens, blocks * tile), jnp.bfloat16),
        compiler_params=pltpu.CompilerParams(vmem_limit_bytes=VMEM_LIMIT),
        cost_estimate=pl.CostEstimate(
            flops=2 * tokens * panels * slots * tile * tile,
            bytes_accessed=2 * (g.size + w.size + tokens * blocks * tile),
            transcendentals=0,
        ),
        name="input_grad",
    )(rows, count, g, w)


def local(tokens, w_tiles, tile_rows, tile_count, grad_hidden):
    panels, slots, tile = w_tiles.shape[1:4]
    width = tokens.shape[1]
    blocks = width // tile
    rows, count, w = tile_rows.reshape(-1), tile_count.reshape(-1), w_tiles[0]

    gathered = lax.all_gather(tokens, "col", axis=0, tiled=True)
    partial_act = forward(rows, count, gathered, w)
    xt = transposed(gathered).reshape(blocks, tile, gathered.shape[0])
    pre_act = lax.psum_scatter(partial_act, "row", scatter_dimension=0, tiled=True)
    pre_act = pre_act.astype(jnp.float32)
    gelu_fn = partial(jax.nn.gelu, approximate=True)
    hidden, backward = jax.vjp(gelu_fn, pre_act)
    grad_pre = backward(grad_hidden.astype(jnp.float32))[0].astype(jnp.bfloat16)
    grad_all = lax.all_gather(grad_pre, "row", axis=0, tiled=True)

    grad_w = weight_grad(rows, count, xt, grad_all, slots, tile)
    grad_w = lax.psum(grad_w, "dp")
    grad_x = input_grad(rows, count, grad_all, w, blocks)
    grad_x = lax.psum_scatter(grad_x, "col", scatter_dimension=0, tiled=True)
    return hidden.astype(jnp.bfloat16), grad_x, grad_w[None]


def solution(mesh):
    return jax.shard_map(
        local,
        mesh=mesh,
        in_specs=(
            P(("dp", "col"), "row"),
            P("row", "col", None, None, None),
            P("row", "col", None),
            P("row", "col"),
            P(("dp", "row"), "col"),
        ),
        out_specs=(
            P(("dp", "row"), "col"),
            P(("dp", "col"), "row"),
            P("row", "col", None, None, None),
        ),
        check_vma=False,
    )
```

```python
from functools import partial

import jax
import jax.numpy as jnp
from jax import lax
from jax.experimental import pallas as pl
from jax.experimental.pallas import tpu as pltpu
from jax.sharding import PartitionSpec as P

VMEM_LIMIT = 24 * 1024 * 1024
RING = 4
COL = RING * RING
ROW = 4


def lanes(start, size):
    return pl.ds(pl.multiple_of(start * size, size), size)


def along_x(value, step):
    pairs = [(i, (i // RING + step) % RING * RING + i % RING) for i in range(COL)]
    return lax.ppermute(value, "col", pairs)


def along_z(value, step):
    pairs = [(i, i // RING * RING + (i % RING + step) % RING) for i in range(COL)]
    return lax.ppermute(value, "col", pairs)


def along_y(value, step):
    size = lax.axis_size("dp")
    return lax.ppermute(value, "dp", [(i, (i + step) % size) for i in range(size)])


def swap_core(value):
    return lax.ppermute(value, "row", [(i, i ^ 1) for i in range(ROW)])


def swap_chip(value):
    return lax.ppermute(value, "row", [(i, i ^ 2) for i in range(ROW)])


def add(*values):
    return sum(v.astype(jnp.float32) for v in values).astype(jnp.bfloat16)


ANY = pl.BlockSpec(memory_space=pl.ANY)
SMEM = pl.BlockSpec(memory_space=pltpu.SMEM)
VMEM = pl.BlockSpec(memory_space=pltpu.VMEM)


def run(copies):
    for copy in copies:
        copy.start()
    for copy in copies:
        copy.wait()


def call(kernel, out_shape, scratch, name, in_specs, out_specs):
    return pl.pallas_call(
        kernel,
        in_specs=in_specs,
        out_specs=out_specs,
        out_shape=out_shape,
        scratch_shapes=scratch,
        compiler_params=pltpu.CompilerParams(vmem_limit_bytes=VMEM_LIMIT),
        cost_estimate=pl.CostEstimate(flops=20_000_000_000, bytes_accessed=0, transcendentals=0),
        name=name,
    )


def live_kernel(count, w_ref, down_ref, across_ref):
    panels, slots, tile, _ = w_ref.shape

    def body(p, carry):
        for k in range(slots):
            block = w_ref[p, k] * (count[p] > k).astype(jnp.bfloat16)
            at = slice(k * tile, (k + 1) * tile)
            down_ref[p, at] = block
            across_ref[p, :, at] = block.T
        return carry

    lax.fori_loop(0, panels, body, 0)


def live_tiles(count, w):
    panels, slots, tile, _ = w.shape
    return call(
        live_kernel,
        [
            jax.ShapeDtypeStruct((panels, slots * tile, tile), jnp.bfloat16),
            jax.ShapeDtypeStruct((panels, tile, slots * tile), jnp.bfloat16),
        ],
        [],
        "live_tiles",
        [SMEM, VMEM],
        [VMEM] * 2,
    )(count, w)


def forward_kernel(layout, rows, place, *refs):
    number = len(layout)
    pieces, (w_ref, keep, send, xt_ref, x_ref, sems) = refs[:number], refs[number:]
    panels, depth, tile = w_ref.shape
    slots = depth // tile
    height = x_ref.shape[0] // RING
    run(
        [
            pltpu.make_async_copy(
                piece,
                x_ref.at[pl.ds(pl.multiple_of(place[i] * height + at, 64), piece.shape[0])],
                sems.at[n],
            )
            for n, (piece, (i, at)) in enumerate(zip(pieces, layout))
        ]
    )
    half = keep.shape[0]
    per_panel = xt_ref.shape[0] // panels

    def body(p, carry):
        weights = w_ref[p]
        for first in range(0, x_ref.shape[0], 256):
            at = slice(first, first + 256)
            chosen = [x_ref[at, lanes(rows[p * slots + k], tile)] for k in range(slots)]
            total = jnp.dot(
                jnp.concatenate(chosen, axis=1), weights, preferred_element_type=jnp.float32
            ).astype(jnp.bfloat16)
            for top in range(first, first + 256, 128):
                out = keep if top < half else send
                out[top % half : top % half + 128, lanes(p, tile)] = total[
                    top - first : top - first + 128
                ]
        for n in range(per_panel):
            block = p * per_panel + n
            xt_ref[block] = x_ref[:, lanes(block, tile)].T
        return carry

    lax.fori_loop(0, panels, body, 0)


def forward(rows, place, steps, w):
    pieces, layout = [], []
    for i, arrays in enumerate(steps):
        at = 0
        for array in arrays:
            pieces.append(array)
            layout.append((i, at))
            at += array.shape[0]
    tokens, width = RING * at, pieces[0].shape[1]
    panels, _, tile = w.shape
    blocks = width // tile
    half = jax.ShapeDtypeStruct((tokens // 2, panels * tile), jnp.bfloat16)
    return call(
        partial(forward_kernel, layout),
        [half, half, jax.ShapeDtypeStruct((blocks, tile, tokens), jnp.bfloat16)],
        [pltpu.VMEM((tokens, width), jnp.bfloat16), pltpu.SemaphoreType.DMA((len(pieces),))],
        "forward",
        [SMEM] * 2 + [ANY] * len(pieces) + [VMEM],
        [VMEM] * 3,
    )(rows, place, *pieces, w)


def input_kernel(layout, rows, count, place, g0, g1, g2, g3, w_ref, *refs):
    outs, (g_ref, sum_ref, sems) = refs[: len(layout)], refs[len(layout) :]
    panels, tile, depth = w_ref.shape
    slots = depth // tile
    height = g0.shape[0]
    run(
        [
            pltpu.make_async_copy(piece, g_ref.at[pl.ds(s * height, height)], sems.at[s])
            for s, piece in enumerate((g0, g1, g2, g3))
        ]
    )
    sum_ref[...] = jnp.zeros_like(sum_ref)
    half = slots // 2

    def body(p, carry):
        live = count[p]

        def spread(first):
            weights = w_ref[p, :, first * tile : (first + half) * tile]
            for top in range(0, g_ref.shape[0], 256):
                at = slice(top, top + 256)
                terms = jnp.dot(
                    g_ref[at, lanes(p, tile)], weights, preferred_element_type=jnp.float32
                )
                for k in range(half):
                    sum_ref[rows[p * slots + first + k], at] += terms[:, k * tile : (k + 1) * tile]

        spread(0)

        @pl.when(live > half)
        def _():
            spread(half)

        return carry

    lax.fori_loop(0, panels, body, 0)
    for out, (i, at) in zip(outs, layout):
        start = pl.multiple_of(place[i] * height + at, 64)
        for r in range(sum_ref.shape[0]):
            out[:, r * tile : (r + 1) * tile] = sum_ref[
                r, pl.ds(start, out.shape[0])
            ].astype(jnp.bfloat16)


def input_grad(rows, count, place, slot_grads, w, blocks, layout):
    panels, tile, _ = w.shape
    height = slot_grads[0].shape[0]
    tokens = RING * height
    outs = [jax.ShapeDtypeStruct((size, blocks * tile), jnp.bfloat16) for _, _, size in layout]
    return call(
        partial(input_kernel, [(i, at) for i, at, _ in layout]),
        outs,
        [
            pltpu.VMEM((tokens, panels * tile), jnp.bfloat16),
            pltpu.VMEM((blocks, tokens, tile), jnp.float32),
            pltpu.SemaphoreType.DMA((RING,)),
        ],
        "input_grad",
        [SMEM] * 3 + [ANY] * RING + [VMEM],
        [VMEM] * len(outs),
    )(rows, count, place, *slot_grads, w)


def weight_kernel(parts, steps, rows, count, mine, *refs):
    xts, pieces = refs[:parts], refs[parts : parts + RING * parts]
    outs, (g_ref, sum_ref, sems) = refs[parts + RING * parts : -3], refs[-3:]
    _, per_step, slots, tile, _ = sum_ref.shape
    half = slots // 2
    copies, at = [], 0
    for n, piece in enumerate(pieces):
        copies.append(
            pltpu.make_async_copy(piece, g_ref.at[pl.ds(at, piece.shape[0])], sems.at[n])
        )
        at += piece.shape[0]
    run(copies)

    def body(out, step, inner, carry):
        panel = lax.rem(mine[0] + step, RING) * per_step + inner
        live = count[panel]

        def product(first):
            total = jnp.zeros((half * tile, tile), jnp.float32)
            at = 0
            for xt in xts:
                chosen = [xt[rows[panel * slots + first + k]] for k in range(half)]
                total += jnp.dot(
                    jnp.concatenate(chosen, axis=0),
                    g_ref[at : at + xt.shape[2], lanes(panel, tile)],
                    preferred_element_type=jnp.float32,
                )
                at += xt.shape[2]
            for k in range(half):
                block = total[k * tile : (k + 1) * tile]
                sum_ref[out, inner, first + k] = jnp.where(
                    live > first + k, block, 0.0
                ).astype(jnp.bfloat16)

        product(0)

        @pl.when(live > half)
        def _():
            product(half)

        @pl.when(live <= half)
        def _():
            sum_ref[out, inner, half:] = jnp.zeros((slots - half, tile, tile), jnp.bfloat16)

        return carry

    copies = [
        pltpu.make_async_copy(sum_ref.at[i], out, sems.at[i]) for i, out in enumerate(outs)
    ]
    for i, copy in enumerate(copies):
        lax.fori_loop(0, per_step, partial(body, i, steps[i]), 0)
        copy.start()
    for copy in copies:
        copy.wait()


def weight_grad(rows, count, mine, xts, pieces, slots, steps):
    blocks, tile, _ = xts[0].shape
    panels = pieces[0].shape[1] // tile
    tokens = sum(piece.shape[0] for piece in pieces)
    quarter = (panels // RING, slots, tile, tile)
    return call(
        partial(weight_kernel, len(xts), steps),
        [jax.ShapeDtypeStruct(quarter, jnp.bfloat16)] * len(steps),
        [
            pltpu.VMEM((tokens, panels * tile), jnp.bfloat16),
            pltpu.VMEM((len(steps),) + quarter, jnp.bfloat16),
            pltpu.SemaphoreType.DMA((len(pieces),)),
        ],
        "weight_grad",
        [SMEM] * 3 + [VMEM] * len(xts) + [ANY] * len(pieces),
        [ANY] * len(steps),
    )(rows, count, mine, *xts, *pieces)


def place_kernel(mine, p0, p1, p2, p3, out, sems):
    size = p0.shape[0]
    run(
        [
            pltpu.make_async_copy(
                piece, out.at[pl.ds(lax.rem(mine[0] + i, RING) * size, size)], sems.at[i]
            )
            for i, piece in enumerate((p0, p1, p2, p3))
        ]
    )


def placed(mine, pieces):
    shape = (RING * pieces[0].shape[0],) + pieces[0].shape[1:]
    return call(
        place_kernel,
        jax.ShapeDtypeStruct(shape, jnp.bfloat16),
        [pltpu.SemaphoreType.DMA((RING,))],
        "placed",
        [SMEM] + [ANY] * RING,
        ANY,
    )(mine, *pieces)


def local(tokens, w_tiles, tile_rows, tile_count, grad_hidden):
    panels, slots, tile = w_tiles.shape[1:4]
    shard, width = tokens.shape
    blocks = width // tile
    rows, count, w = tile_rows.reshape(-1), tile_count.reshape(-1), w_tiles[0]
    at = lax.axis_index("col")
    at_x, at_z = at // RING, at % RING
    row = lax.axis_index("row")
    mine = lax.axis_index("dp").astype(jnp.int32).reshape(1)

    seen = jnp.bitwise_xor((at_x + jnp.arange(RING)) % RING, row)
    slot_of_step = ((seen % 2) * 2 + seen // 2).astype(jnp.int32)

    gelu_fn = partial(jax.nn.gelu, approximate=True)
    hold = lax.optimization_barrier

    def into_rows(keep, send):
        half = keep.astype(jnp.float32) + send.astype(jnp.float32)
        height = half.shape[0] // 2
        return half[:height], half[height:].astype(jnp.bfloat16)

    def activate(members, ours, theirs):
        pre_act = ours + theirs.astype(jnp.float32)
        act, backward = jax.vjp(gelu_fn, pre_act)
        cotangent = [
            lax.dynamic_slice_in_dim(grad_hidden, (at_z + j) % RING * shard, shard) for j in members
        ]
        cotangent = jnp.concatenate(cotangent, axis=0).astype(jnp.float32)
        return act.astype(jnp.bfloat16), backward(cotangent)[0].astype(jnp.bfloat16)

    own = tokens
    z1, z3 = along_z(own, -1), along_z(own, 1)
    x1, x3, x2 = along_x(own, -1), along_x(own, 1), along_x(own, 2)
    down, across = live_tiles(count, w)
    z1, z3, x1, x3, x2, own, down, across = hold((z1, z3, x1, x3, x2, own, down, across))

    both = jnp.concatenate([z1, z3], axis=0)
    both1, both3 = along_x(both, -1), along_x(both, 1)
    z2 = along_z(own, 2)
    keep0, send0, xt0 = forward(rows, slot_of_step, ([own], [x1], [x2], [x3]), down)
    both, both1, both3, z2, keep0, send0, xt0 = hold((both, both1, both3, z2, keep0, send0, xt0))

    z1x2, z3x2 = along_x(both3[:shard], 1), along_x(both1[shard:], -1)
    z2x1, z2x3 = along_x(z2, -1), along_x(z2, 1)
    ours0, theirs0 = into_rows(keep0, swap_core(send0))
    theirs0 = swap_chip(theirs0)
    z1x2, z3x2, z2x1, z2x3, theirs0 = hold((z1x2, z3x2, z2x1, z2x3, theirs0))
    z2x2 = along_x(z2, 2)
    keep1, send1, xt1 = forward(
        rows, slot_of_step, ([both], [both1], [z1x2, z3x2], [both3]), down
    )
    z2x2, send1, theirs0 = hold((z2x2, send1, theirs0))

    act0, grad0 = activate((0,), ours0, theirs0)
    ours1, theirs1 = into_rows(keep1, swap_core(send1))
    theirs1, grad0, z2x2 = hold((theirs1, grad0, z2x2))
    theirs1, other0 = swap_chip(theirs1), swap_chip(grad0)
    keep2, send2, xt2 = forward(rows, slot_of_step, ([z2], [z2x1], [z2x2], [z2x3]), down)
    ours2, theirs2 = into_rows(keep2, swap_core(send2))
    theirs2, slots0 = hold((theirs2, [grad0, other0, swap_core(grad0), swap_core(other0)]))
    theirs2 = swap_chip(theirs2)
    split = partial(input_grad, rows, count, slot_of_step, w=across, blocks=blocks)
    single = [(i, 0, shard) for i in range(RING)]
    double = [(0, 0, 2 * shard), (1, 0, 2 * shard), (2, 0, shard), (2, shard, shard), (3, 0, 2 * shard)]
    p0 = split(slots0, layout=single)
    theirs1, p0 = hold((theirs1, p0))

    act1, grad1 = activate((1, 3), ours1, theirs1)
    grad1, theirs2 = hold((grad1, theirs2))
    other1, grad1c = swap_chip(grad1), swap_core(grad1)
    act2, grad2 = activate((2,), ours2, theirs2)
    other1, grad1c, grad2 = hold((other1, grad1c, grad2))
    other2 = swap_chip(grad2)
    near1, near3, near2 = along_x(p0[1], 1), along_x(p0[3], -1), along_x(p0[2], 2)
    slots1 = [grad1, other1, grad1c, swap_core(other1)]
    a0, a1, a2, a3, a4 = split(slots1, layout=double)
    grad2c = swap_core(grad2)
    a2, a3, near1, near2, near3, grad2c, other2 = hold((a2, a3, near1, near2, near3, grad2c, other2))

    up, dn = along_x(a2, 1), along_x(a3, -1)
    slots2 = [grad2, other2, grad2c, swap_core(other2)]
    p2 = split(slots2, layout=single)
    up, dn, p2 = hold((up, dn, p2))
    far2 = along_x(p2[2], 2)
    up = along_x(jnp.concatenate([add(a1[:shard], up), a1[shard:], p2[1]], axis=0), 1)
    dn = along_x(jnp.concatenate([a4[:shard], add(a4[shard:], dn), p2[3]], axis=0), -1)
    weights = partial(
        weight_grad, rows, count, mine, pieces=slots0 + slots1 + slots2, slots=slots
    )
    q1, q3 = weights((xt0, xt1, xt2), steps=(1, 3))
    q1, q3, xt0, xt1, xt2 = hold((q1, q3, xt0, xt1, xt2))
    q1, q3 = along_y(q1, 1), along_y(q3, -1)
    q2, q0 = weights((xt0, xt1, xt2), steps=(2, 0))
    q2 = along_y(q2, 2)
    near = add(p0[0], near1, near3, near2)
    hidden = jnp.zeros(grad_hidden.shape, jnp.bfloat16)
    for j, act in ((0, act0), (1, act1[:shard]), (3, act1[shard:]), (2, act2)):
        hidden = lax.dynamic_update_slice(hidden, act, ((at_z + j) % RING * shard, 0))
    up, dn, near, hidden = hold((up, dn, near, hidden))

    ahead = add(a0[:shard], up[:shard], dn[:shard])
    behind = add(a0[shard:], up[shard : 2 * shard], dn[shard : 2 * shard])
    far = add(p2[0], up[2 * shard :], dn[2 * shard :], far2)
    ahead, behind, far = hold((ahead, behind, far))
    q1, q3, q2, ahead = hold((q1, q3, q2, ahead))
    ahead, behind, far = along_z(ahead, 1), along_z(behind, -1), along_z(far, 2)
    quarter = add(q0, q1, q3, q2)
    q1, q3, q2 = along_y(quarter, -1), along_y(quarter, 1), along_y(quarter, 2)
    grad_x = add(near, far, ahead, behind)
    grad_w = placed(mine, [quarter, q1, q2, q3])
    return hidden, grad_x, grad_w[None]


def solution(mesh):
    return jax.shard_map(
        local,
        mesh=mesh,
        in_specs=(
            P(("dp", "col"), "row"),
            P("row", "col", None, None, None),
            P("row", "col", None),
            P("row", "col"),
            P(("dp", "row"), "col"),
        ),
        out_specs=(
            P(("dp", "row"), "col"),
            P(("dp", "col"), "row"),
            P("row", "col", None, None, None),
        ),
        check_vma=False,
    )
```

```python
from functools import partial

import jax
import jax.numpy as jnp
from jax import lax
from jax.experimental import pallas as pl
from jax.experimental.pallas import tpu as pltpu
from jax.sharding import PartitionSpec as P

VMEM_LIMIT = 24 * 1024 * 1024
RING = 4
COL = RING * RING
ROW = 4


def lanes(start, size):
    return pl.ds(pl.multiple_of(start * size, size), size)


def along_x(value, step):
    pairs = [(i, (i // RING + step) % RING * RING + i % RING) for i in range(COL)]
    return lax.ppermute(value, "col", pairs)


def along_z(value, step):
    pairs = [(i, i // RING * RING + (i % RING + step) % RING) for i in range(COL)]
    return lax.ppermute(value, "col", pairs)


def along_y(value, step):
    size = lax.axis_size("dp")
    return lax.ppermute(value, "dp", [(i, (i + step) % size) for i in range(size)])


def swap_core(value):
    return lax.ppermute(value, "row", [(i, i ^ 1) for i in range(ROW)])


def swap_chip(value):
    return lax.ppermute(value, "row", [(i, i ^ 2) for i in range(ROW)])


def add(*values):
    return sum(v.astype(jnp.float32) for v in values).astype(jnp.bfloat16)


ANY = pl.BlockSpec(memory_space=pl.ANY)
SMEM = pl.BlockSpec(memory_space=pltpu.SMEM)
VMEM = pl.BlockSpec(memory_space=pltpu.VMEM)


def run(copies):
    for copy in copies:
        copy.start()
    for copy in copies:
        copy.wait()


def call(kernel, out_shape, scratch, name, in_specs, out_specs, flops=20_000_000_000):
    return pl.pallas_call(
        kernel,
        in_specs=in_specs,
        out_specs=out_specs,
        out_shape=out_shape,
        scratch_shapes=scratch,
        compiler_params=pltpu.CompilerParams(vmem_limit_bytes=VMEM_LIMIT),
        cost_estimate=pl.CostEstimate(flops=flops, bytes_accessed=0, transcendentals=0),
        name=name,
    )


def live_kernel(count, w_ref, down_ref, across_ref):
    panels, slots, tile, _ = w_ref.shape

    def body(p, carry):
        for k in range(slots):
            block = w_ref[p, k] * (count[p] > k).astype(jnp.bfloat16)
            at = slice(k * tile, (k + 1) * tile)
            down_ref[p, at] = block
            across_ref[p, :, at] = block.T
        return carry

    lax.fori_loop(0, panels, body, 0)


def live_tiles(count, w):
    panels, slots, tile, _ = w.shape
    return call(
        live_kernel,
        [
            jax.ShapeDtypeStruct((panels, slots * tile, tile), jnp.bfloat16),
            jax.ShapeDtypeStruct((panels, tile, slots * tile), jnp.bfloat16),
        ],
        [],
        "live_tiles",
        [SMEM, VMEM],
        [VMEM] * 2,
    )(count, w)


def forward_kernel(layout, rows, place, *refs):
    number = len(layout)
    pieces, (w_ref, keep, send, xt_ref, x_ref, sems) = refs[:number], refs[number:]
    panels, depth, tile = w_ref.shape
    slots = depth // tile
    height = x_ref.shape[0] // RING
    run(
        [
            pltpu.make_async_copy(
                piece,
                x_ref.at[pl.ds(pl.multiple_of(place[i] * height + at, 64), piece.shape[0])],
                sems.at[n],
            )
            for n, (piece, (i, at)) in enumerate(zip(pieces, layout))
        ]
    )
    half = keep.shape[0]
    per_panel = xt_ref.shape[0] // panels

    def body(p, carry):
        weights = w_ref[p]
        for first in range(0, x_ref.shape[0], 256):
            at = slice(first, first + 256)
            chosen = [x_ref[at, lanes(rows[p * slots + k], tile)] for k in range(slots)]
            total = jnp.dot(
                jnp.concatenate(chosen, axis=1), weights, preferred_element_type=jnp.float32
            ).astype(jnp.bfloat16)
            for top in range(first, first + 256, 128):
                out = keep if top < half else send
                out[top % half : top % half + 128, lanes(p, tile)] = total[
                    top - first : top - first + 128
                ]
        for n in range(per_panel):
            block = p * per_panel + n
            xt_ref[block] = x_ref[:, lanes(block, tile)].T
        return carry

    lax.fori_loop(0, panels, body, 0)


def forward(rows, place, steps, w, **cost):
    pieces, layout = [], []
    for i, arrays in enumerate(steps):
        at = 0
        for array in arrays:
            pieces.append(array)
            layout.append((i, at))
            at += array.shape[0]
    tokens, width = RING * at, pieces[0].shape[1]
    panels, _, tile = w.shape
    blocks = width // tile
    half = jax.ShapeDtypeStruct((tokens // 2, panels * tile), jnp.bfloat16)
    return call(
        partial(forward_kernel, layout),
        [half, half, jax.ShapeDtypeStruct((blocks, tile, tokens), jnp.bfloat16)],
        [pltpu.VMEM((tokens, width), jnp.bfloat16), pltpu.SemaphoreType.DMA((len(pieces),))],
        "forward",
        [SMEM] * 2 + [ANY] * len(pieces) + [VMEM],
        [VMEM] * 3,
        **cost,
    )(rows, place, *pieces, w)


def input_kernel(layout, rows, count, place, g0, g1, g2, g3, w_ref, *refs):
    outs, (g_ref, sum_ref, sems) = refs[: len(layout)], refs[len(layout) :]
    panels, tile, depth = w_ref.shape
    slots = depth // tile
    height = g0.shape[0]
    run(
        [
            pltpu.make_async_copy(piece, g_ref.at[pl.ds(s * height, height)], sems.at[s])
            for s, piece in enumerate((g0, g1, g2, g3))
        ]
    )
    sum_ref[...] = jnp.zeros_like(sum_ref)
    half = slots // 2

    def body(p, carry):
        live = count[p]

        def spread(first):
            weights = w_ref[p, :, first * tile : (first + half) * tile]
            for top in range(0, g_ref.shape[0], 256):
                at = slice(top, top + 256)
                terms = jnp.dot(
                    g_ref[at, lanes(p, tile)], weights, preferred_element_type=jnp.float32
                )
                for k in range(half):
                    sum_ref[rows[p * slots + first + k], at] += terms[:, k * tile : (k + 1) * tile]

        spread(0)

        @pl.when(live > half)
        def _():
            spread(half)

        return carry

    lax.fori_loop(0, panels, body, 0)
    for out, (i, at) in zip(outs, layout):
        start = pl.multiple_of(place[i] * height + at, 64)
        for r in range(sum_ref.shape[0]):
            out[:, r * tile : (r + 1) * tile] = sum_ref[
                r, pl.ds(start, out.shape[0])
            ].astype(jnp.bfloat16)


def input_grad(rows, count, place, slot_grads, w, blocks, layout):
    panels, tile, _ = w.shape
    height = slot_grads[0].shape[0]
    tokens = RING * height
    outs = [jax.ShapeDtypeStruct((size, blocks * tile), jnp.bfloat16) for _, _, size in layout]
    return call(
        partial(input_kernel, [(i, at) for i, at, _ in layout]),
        outs,
        [
            pltpu.VMEM((tokens, panels * tile), jnp.bfloat16),
            pltpu.VMEM((blocks, tokens, tile), jnp.float32),
            pltpu.SemaphoreType.DMA((RING,)),
        ],
        "input_grad",
        [SMEM] * 3 + [ANY] * RING + [VMEM],
        [VMEM] * len(outs),
    )(rows, count, place, *slot_grads, w)


def weight_kernel(parts, steps, rows, count, mine, *refs):
    xts, pieces = refs[:parts], refs[parts : parts + RING * parts]
    outs, (g_ref, sum_ref, sems) = refs[parts + RING * parts : -3], refs[-3:]
    _, per_step, slots, tile, _ = sum_ref.shape
    half = slots // 2
    copies, at = [], 0
    for n, piece in enumerate(pieces):
        copies.append(
            pltpu.make_async_copy(piece, g_ref.at[pl.ds(at, piece.shape[0])], sems.at[n])
        )
        at += piece.shape[0]
    run(copies)

    def body(out, step, inner, carry):
        panel = lax.rem(mine[0] + step, RING) * per_step + inner
        live = count[panel]

        def product(first):
            total = jnp.zeros((half * tile, tile), jnp.float32)
            at = 0
            for xt in xts:
                chosen = [xt[rows[panel * slots + first + k]] for k in range(half)]
                total += jnp.dot(
                    jnp.concatenate(chosen, axis=0),
                    g_ref[at : at + xt.shape[2], lanes(panel, tile)],
                    preferred_element_type=jnp.float32,
                )
                at += xt.shape[2]
            for k in range(half):
                block = total[k * tile : (k + 1) * tile]
                sum_ref[out, inner, first + k] = jnp.where(
                    live > first + k, block, 0.0
                ).astype(jnp.bfloat16)

        product(0)

        @pl.when(live > half)
        def _():
            product(half)

        @pl.when(live <= half)
        def _():
            sum_ref[out, inner, half:] = jnp.zeros((slots - half, tile, tile), jnp.bfloat16)

        return carry

    copies, done = [], 0
    for i, step in enumerate(steps):
        lax.fori_loop(0, per_step, partial(body, i, step), 0)
        at = 0
        while at < slots:
            out = outs[done]
            copies.append(
                pltpu.make_async_copy(
                    sum_ref.at[i, :, pl.ds(at, out.shape[1])], out, sems.at[done]
                )
            )
            copies[-1].start()
            at, done = at + out.shape[1], done + 1
    for copy in copies:
        copy.wait()


def weight_grad(rows, count, mine, xts, pieces, slots, steps, cut=1, **cost):
    blocks, tile, _ = xts[0].shape
    panels = pieces[0].shape[1] // tile
    tokens = sum(piece.shape[0] for piece in pieces)
    quarter = (panels // RING, slots, tile, tile)
    return call(
        partial(weight_kernel, len(xts), steps),
        [jax.ShapeDtypeStruct((panels // RING, slots // cut, tile, tile), jnp.bfloat16)]
        * (cut * len(steps)),
        [
            pltpu.VMEM((tokens, panels * tile), jnp.bfloat16),
            pltpu.VMEM((len(steps),) + quarter, jnp.bfloat16),
            pltpu.SemaphoreType.DMA((len(pieces),)),
        ],
        "weight_grad",
        [SMEM] * 3 + [VMEM] * len(xts) + [ANY] * len(pieces),
        [ANY] * (cut * len(steps)),
        **cost,
    )(rows, count, mine, *xts, *pieces)


def place_kernel(mine, p0, p1, p2, p3, out, sems):
    size = p0.shape[0]
    run(
        [
            pltpu.make_async_copy(
                piece, out.at[pl.ds(lax.rem(mine[0] + i, RING) * size, size)], sems.at[i]
            )
            for i, piece in enumerate((p0, p1, p2, p3))
        ]
    )


def placed(mine, pieces):
    shape = (RING * pieces[0].shape[0],) + pieces[0].shape[1:]
    return call(
        place_kernel,
        jax.ShapeDtypeStruct(shape, jnp.bfloat16),
        [pltpu.SemaphoreType.DMA((RING,))],
        "placed",
        [SMEM] + [ANY] * RING,
        ANY,
    )(mine, *pieces)


def local(tokens, w_tiles, tile_rows, tile_count, grad_hidden):
    panels, slots, tile = w_tiles.shape[1:4]
    shard, width = tokens.shape
    blocks = width // tile
    rows, count, w = tile_rows.reshape(-1), tile_count.reshape(-1), w_tiles[0]
    at = lax.axis_index("col")
    at_x, at_z = at // RING, at % RING
    row = lax.axis_index("row")
    mine = lax.axis_index("dp").astype(jnp.int32).reshape(1)

    seen = jnp.bitwise_xor((at_x + jnp.arange(RING)) % RING, row)
    slot_of_step = ((seen % 2) * 2 + seen // 2).astype(jnp.int32)

    gelu_fn = partial(jax.nn.gelu, approximate=True)
    hold = lax.optimization_barrier

    def into_rows(keep, send):
        half = keep.astype(jnp.float32) + send.astype(jnp.float32)
        height = half.shape[0] // 2
        return half[:height], half[height:].astype(jnp.bfloat16)

    def activate(members, ours, theirs):
        pre_act = ours + theirs.astype(jnp.float32)
        act, backward = jax.vjp(gelu_fn, pre_act)
        cotangent = [
            lax.dynamic_slice_in_dim(grad_hidden, (at_z + j) % RING * shard, shard) for j in members
        ]
        cotangent = jnp.concatenate(cotangent, axis=0).astype(jnp.float32)
        return act.astype(jnp.bfloat16), backward(cotangent)[0].astype(jnp.bfloat16)

    own = tokens
    x1, x3, x2 = along_x(own, -1), along_x(own, 1), along_x(own, 2)
    z1, z3 = along_z(own, -1), along_z(own, 1)
    down, across = live_tiles(count, w)
    z1, z3, x1, x3, x2, own, down, across = hold((z1, z3, x1, x3, x2, own, down, across))

    both = jnp.concatenate([z1, z3], axis=0)
    both1, both3 = along_x(both, -1), along_x(both, 1)
    z2 = along_z(own, 2)
    keep0, send0, xt0 = forward(
        rows, slot_of_step, ([own], [x1], [x2], [x3]), down, flops=1_000_000_000
    )
    both, both1, both3, z2, x2, keep0, send0, xt0 = hold(
        (both, both1, both3, z2, x2, keep0, send0, xt0)
    )

    z1x2, z3x2 = along_x(both3[:shard], 1), along_x(both1[shard:], -1)
    z2x1, z2x3 = along_x(z2, -1), along_x(z2, 1)
    ours0, theirs0 = into_rows(keep0, swap_core(send0))
    theirs0 = swap_chip(theirs0)
    z1x2, z3x2, z2x1, z2x3, theirs0 = hold((z1x2, z3x2, z2x1, z2x3, theirs0))
    z2x2 = along_x(z2, 2)
    keep1, send1, xt1 = forward(
        rows, slot_of_step, ([both], [both1], [z1x2, z3x2], [both3]), down
    )
    z2x2, send1, theirs0 = hold((z2x2, send1, theirs0))

    act0, grad0 = activate((0,), ours0, theirs0)
    ours1, theirs1 = into_rows(keep1, swap_core(send1))
    theirs1, grad0, z2x2 = hold((theirs1, grad0, z2x2))
    theirs1, other0 = swap_chip(theirs1), swap_chip(grad0)
    keep2, send2, xt2 = forward(rows, slot_of_step, ([z2], [z2x1], [z2x2], [z2x3]), down)
    theirs1, other0, keep2, send2 = hold((theirs1, other0, keep2, send2))
    ours2, theirs2 = into_rows(keep2, swap_core(send2))
    act1, grad1 = activate((1, 3), ours1, theirs1)
    grad1, theirs2 = hold((grad1, theirs2))

    other1, theirs2 = swap_chip(grad1), swap_chip(theirs2)
    grad1c = swap_core(grad1)
    slots0 = [grad0, other0, swap_core(grad0), swap_core(other0)]
    theirs2, grad1c, slots0 = hold((theirs2, grad1c, slots0))
    act2, grad2 = activate((2,), ours2, theirs2)
    grad2, slots0 = hold((grad2, slots0))
    other2, grad2c = swap_chip(grad2), swap_core(grad2)
    split = partial(input_grad, rows, count, slot_of_step, w=across, blocks=blocks)
    single = [(i, 0, shard) for i in range(RING)]
    double = [(0, 0, 2 * shard), (1, 0, 2 * shard), (2, 0, shard), (2, shard, shard), (3, 0, 2 * shard)]
    p0 = split(slots0, layout=single)
    other1, grad2c, p0 = hold((other1, grad2c, p0))
    near1, near3, near2 = along_x(p0[1], 1), along_x(p0[3], -1), along_x(p0[2], 2)
    slots1 = [grad1, other1, grad1c, swap_core(other1)]
    a0, a1, a2, a3, a4 = split(slots1, layout=double)
    slots2 = [grad2, other2, grad2c, swap_core(other2)]
    a2, a3, slots2 = hold((a2, a3, slots2))

    up, dn = along_x(a2, 1), along_x(a3, -1)
    weights = partial(
        weight_grad, rows, count, mine, pieces=slots0 + slots1 + slots2, slots=slots
    )
    q2, q2h = weights((xt0, xt1, xt2), steps=(2,), cut=2)
    q2, q2h, slots2, near1, near2, near3 = hold((q2, q2h, slots2, near1, near2, near3))
    q2, q2h = along_y(q2, 1), along_y(q2h, -1)
    p2 = split(slots2, layout=single)
    up, dn, p2, xt0, xt1, xt2 = hold((up, dn, p2, xt0, xt1, xt2))
    far1, far3, far2 = along_x(p2[1], 1), along_x(p2[3], -1), along_x(p2[2], 2)
    up = jnp.concatenate([add(a1[:shard], up), a1[shard:]], axis=0)
    dn = jnp.concatenate([a4[:shard], add(a4[shard:], dn)], axis=0)
    near = add(p0[0], near1, near3, near2)
    q1, q3, q0 = weights((xt0, xt1, xt2), steps=(1, 3, 0), flops=100_000_000)
    q1, q3, q2, q2h, q0, up, dn, near = hold((q1, q3, q2, q2h, q0, up, dn, near))
    half = slots // 2
    q1 = along_y(jnp.concatenate([add(q1[:, :half], q2), q1[:, half:]], axis=1), 1)
    q3 = along_y(jnp.concatenate([q3[:, :half], add(q3[:, half:], q2h)], axis=1), -1)
    up, dn = along_x(up, 1), along_x(dn, -1)
    far1, far3, far2, q0 = hold((far1, far3, far2, q0))
    far = along_z(add(p2[0], far1, far3, far2), 2)
    hidden = jnp.zeros(grad_hidden.shape, jnp.bfloat16)
    for j, act in ((0, act0), (1, act1[:shard]), (3, act1[shard:]), (2, act2)):
        hidden = lax.dynamic_update_slice(hidden, act, ((at_z + j) % RING * shard, 0))
    q1, q3, hidden = hold((q1, q3, hidden))

    quarter = add(q0, q1, q3)
    quarter, up, dn = hold((quarter, up, dn))
    ahead, behind = add(a0[:shard], up[:shard], dn[:shard]), add(a0[shard:], up[shard:], dn[shard:])
    ahead, behind = along_z(ahead, 1), along_z(behind, -1)
    q1, q3, q2 = along_y(quarter, -1), along_y(quarter, 1), along_y(quarter, 2)
    grad_x = add(near, far, ahead, behind)
    grad_w = placed(mine, [quarter, q1, q2, q3])
    return hidden, grad_x, grad_w[None]


def solution(mesh):
    return jax.shard_map(
        local,
        mesh=mesh,
        in_specs=(
            P(("dp", "col"), "row"),
            P("row", "col", None, None, None),
            P("row", "col", None),
            P("row", "col"),
            P(("dp", "row"), "col"),
        ),
        out_specs=(
            P(("dp", "row"), "col"),
            P(("dp", "col"), "row"),
            P("row", "col", None, None, None),
        ),
        check_vma=False,
    )
```

```python
from functools import partial

import jax
import jax.numpy as jnp
from jax import lax
from jax.experimental import pallas as pl
from jax.experimental.pallas import tpu as pltpu
from jax.sharding import PartitionSpec as P

VMEM_LIMIT = 24 * 1024 * 1024
RING = 4
COL = RING * RING
ROW = 4


def lanes(start, size):
    return pl.ds(pl.multiple_of(start * size, size), size)


def along_x(value, step):
    pairs = [(i, (i // RING + step) % RING * RING + i % RING) for i in range(COL)]
    return lax.ppermute(value, "col", pairs)


def along_z(value, step):
    pairs = [(i, i // RING * RING + (i % RING + step) % RING) for i in range(COL)]
    return lax.ppermute(value, "col", pairs)


def along_y(value, step):
    size = lax.axis_size("dp")
    return lax.ppermute(value, "dp", [(i, (i + step) % size) for i in range(size)])


def swap_core(value):
    return lax.ppermute(value, "row", [(i, i ^ 1) for i in range(ROW)])


def swap_chip(value):
    return lax.ppermute(value, "row", [(i, i ^ 2) for i in range(ROW)])


def add(*values):
    return sum(v.astype(jnp.float32) for v in values).astype(jnp.bfloat16)


ANY = pl.BlockSpec(memory_space=pl.ANY)
SMEM = pl.BlockSpec(memory_space=pltpu.SMEM)
VMEM = pl.BlockSpec(memory_space=pltpu.VMEM)


def run(copies):
    for copy in copies:
        copy.start()
    for copy in copies:
        copy.wait()


def call(kernel, out_shape, scratch, name, in_specs, out_specs, flops=20_000_000_000):
    return pl.pallas_call(
        kernel,
        in_specs=in_specs,
        out_specs=out_specs,
        out_shape=out_shape,
        scratch_shapes=scratch,
        compiler_params=pltpu.CompilerParams(vmem_limit_bytes=VMEM_LIMIT),
        cost_estimate=pl.CostEstimate(flops=flops, bytes_accessed=0, transcendentals=0),
        name=name,
    )


def live_kernel(count, w_ref, down_ref, across_ref):
    panels, slots, tile, _ = w_ref.shape

    def body(p, carry):
        for k in range(slots):
            block = w_ref[p, k] * (count[p] > k).astype(jnp.bfloat16)
            at = slice(k * tile, (k + 1) * tile)
            down_ref[p, at] = block
            across_ref[p, :, at] = block.T
        return carry

    lax.fori_loop(0, panels, body, 0)


def live_tiles(count, w):
    panels, slots, tile, _ = w.shape
    return call(
        live_kernel,
        [
            jax.ShapeDtypeStruct((panels, slots * tile, tile), jnp.bfloat16),
            jax.ShapeDtypeStruct((panels, tile, slots * tile), jnp.bfloat16),
        ],
        [],
        "live_tiles",
        [SMEM, VMEM],
        [VMEM] * 2,
    )(count, w)


def forward_kernel(layout, rows, place, *refs):
    number = len(layout)
    pieces, (w_ref, keep, send, xt_ref, x_ref, sems) = refs[:number], refs[number:]
    panels, depth, tile = w_ref.shape
    slots = depth // tile
    height = x_ref.shape[0] // RING
    run(
        [
            pltpu.make_async_copy(
                piece,
                x_ref.at[pl.ds(pl.multiple_of(place[i] * height + at, 64), piece.shape[0])],
                sems.at[n],
            )
            for n, (piece, (i, at)) in enumerate(zip(pieces, layout))
        ]
    )
    half = keep.shape[0]
    per_panel = xt_ref.shape[0] // panels

    def body(p, carry):
        weights = w_ref[p]
        for first in range(0, x_ref.shape[0], 256):
            at = slice(first, first + 256)
            chosen = [x_ref[at, lanes(rows[p * slots + k], tile)] for k in range(slots)]
            total = jnp.dot(
                jnp.concatenate(chosen, axis=1), weights, preferred_element_type=jnp.float32
            ).astype(jnp.bfloat16)
            for top in range(first, first + 256, 128):
                out = keep if top < half else send
                out[top % half : top % half + 128, lanes(p, tile)] = total[
                    top - first : top - first + 128
                ]
        for n in range(per_panel):
            block = p * per_panel + n
            xt_ref[block] = x_ref[:, lanes(block, tile)].T
        return carry

    lax.fori_loop(0, panels, body, 0)


def forward(rows, place, steps, w, **cost):
    pieces, layout = [], []
    for i, arrays in enumerate(steps):
        at = 0
        for array in arrays:
            pieces.append(array)
            layout.append((i, at))
            at += array.shape[0]
    tokens, width = RING * at, pieces[0].shape[1]
    panels, _, tile = w.shape
    blocks = width // tile
    half = jax.ShapeDtypeStruct((tokens // 2, panels * tile), jnp.bfloat16)
    return call(
        partial(forward_kernel, layout),
        [half, half, jax.ShapeDtypeStruct((blocks, tile, tokens), jnp.bfloat16)],
        [pltpu.VMEM((tokens, width), jnp.bfloat16), pltpu.SemaphoreType.DMA((len(pieces),))],
        "forward",
        [SMEM] * 2 + [ANY] * len(pieces) + [VMEM],
        [VMEM] * 3,
        **cost,
    )(rows, place, *pieces, w)


def input_kernel(layout, rows, count, place, g0, g1, g2, g3, w_ref, *refs):
    outs, (g_ref, sum_ref, sems) = refs[: len(layout)], refs[len(layout) :]
    panels, tile, depth = w_ref.shape
    slots = depth // tile
    height = g0.shape[0]
    run(
        [
            pltpu.make_async_copy(piece, g_ref.at[pl.ds(s * height, height)], sems.at[s])
            for s, piece in enumerate((g0, g1, g2, g3))
        ]
    )
    sum_ref[...] = jnp.zeros_like(sum_ref)
    half = slots // 2

    def body(p, carry):
        live = count[p]

        def spread(first):
            weights = w_ref[p, :, first * tile : (first + half) * tile]
            for top in range(0, g_ref.shape[0], 256):
                at = slice(top, top + 256)
                terms = jnp.dot(
                    g_ref[at, lanes(p, tile)], weights, preferred_element_type=jnp.float32
                )
                for k in range(half):
                    sum_ref[rows[p * slots + first + k], at] += terms[:, k * tile : (k + 1) * tile]

        spread(0)

        @pl.when(live > half)
        def _():
            spread(half)

        return carry

    lax.fori_loop(0, panels, body, 0)
    for out, (i, at) in zip(outs, layout):
        start = pl.multiple_of(place[i] * height + at, 64)
        for r in range(sum_ref.shape[0]):
            out[:, r * tile : (r + 1) * tile] = sum_ref[
                r, pl.ds(start, out.shape[0])
            ].astype(jnp.bfloat16)


def input_grad(rows, count, place, slot_grads, w, blocks, layout):
    panels, tile, _ = w.shape
    height = slot_grads[0].shape[0]
    tokens = RING * height
    outs = [jax.ShapeDtypeStruct((size, blocks * tile), jnp.bfloat16) for _, _, size in layout]
    return call(
        partial(input_kernel, [(i, at) for i, at, _ in layout]),
        outs,
        [
            pltpu.VMEM((tokens, panels * tile), jnp.bfloat16),
            pltpu.VMEM((blocks, tokens, tile), jnp.float32),
            pltpu.SemaphoreType.DMA((RING,)),
        ],
        "input_grad",
        [SMEM] * 3 + [ANY] * RING + [VMEM],
        [VMEM] * len(outs),
    )(rows, count, place, *slot_grads, w)


def weight_kernel(parts, steps, rows, count, mine, *refs):
    xts, pieces = refs[:parts], refs[parts : parts + RING * parts]
    outs, (g_ref, sum_ref, sems) = refs[parts + RING * parts : -3], refs[-3:]
    _, per_step, slots, tile, _ = sum_ref.shape
    half = slots // 2
    copies, width = [], per_step * tile
    for step in steps:
        at = 0
        used = pl.ds(pl.multiple_of(lax.rem(mine[0] + step, RING) * width, width), width)
        for piece in pieces:
            copies.append(
                pltpu.make_async_copy(
                    piece.at[:, used],
                    g_ref.at[pl.ds(at, piece.shape[0]), used],
                    sems.at[len(copies)],
                )
            )
            at += piece.shape[0]
    run(copies)

    def body(out, step, inner, carry):
        panel = lax.rem(mine[0] + step, RING) * per_step + inner
        live = count[panel]

        def product(first):
            total = jnp.zeros((half * tile, tile), jnp.float32)
            at = 0
            for xt in xts:
                chosen = [xt[rows[panel * slots + first + k]] for k in range(half)]
                total += jnp.dot(
                    jnp.concatenate(chosen, axis=0),
                    g_ref[at : at + xt.shape[2], lanes(panel, tile)],
                    preferred_element_type=jnp.float32,
                )
                at += xt.shape[2]
            for k in range(half):
                block = total[k * tile : (k + 1) * tile]
                sum_ref[out, inner, first + k] = jnp.where(
                    live > first + k, block, 0.0
                ).astype(jnp.bfloat16)

        product(0)

        @pl.when(live > half)
        def _():
            product(half)

        @pl.when(live <= half)
        def _():
            sum_ref[out, inner, half:] = jnp.zeros((slots - half, tile, tile), jnp.bfloat16)

        return carry

    copies, done = [], 0
    for i, step in enumerate(steps):
        lax.fori_loop(0, per_step, partial(body, i, step), 0)
        at = 0
        while at < slots:
            out = outs[done]
            copies.append(
                pltpu.make_async_copy(
                    sum_ref.at[i, :, pl.ds(at, out.shape[1])], out, sems.at[done]
                )
            )
            copies[-1].start()
            at, done = at + out.shape[1], done + 1
    for copy in copies:
        copy.wait()


def weight_grad(rows, count, mine, xts, pieces, slots, steps, cut=1, **cost):
    blocks, tile, _ = xts[0].shape
    panels = pieces[0].shape[1] // tile
    tokens = sum(piece.shape[0] for piece in pieces)
    quarter = (panels // RING, slots, tile, tile)
    return call(
        partial(weight_kernel, len(xts), steps),
        [jax.ShapeDtypeStruct((panels // RING, slots // cut, tile, tile), jnp.bfloat16)]
        * (cut * len(steps)),
        [
            pltpu.VMEM((tokens, panels * tile), jnp.bfloat16),
            pltpu.VMEM((len(steps),) + quarter, jnp.bfloat16),
            pltpu.SemaphoreType.DMA((len(pieces) * len(steps),)),
        ],
        "weight_grad",
        [SMEM] * 3 + [VMEM] * len(xts) + [ANY] * len(pieces),
        [ANY] * (cut * len(steps)),
        **cost,
    )(rows, count, mine, *xts, *pieces)


def place_kernel(mine, p0, p1, p2, p3, out, sems):
    size = p0.shape[0]
    run(
        [
            pltpu.make_async_copy(
                piece, out.at[pl.ds(lax.rem(mine[0] + i, RING) * size, size)], sems.at[i]
            )
            for i, piece in enumerate((p0, p1, p2, p3))
        ]
    )


def placed(mine, pieces):
    shape = (RING * pieces[0].shape[0],) + pieces[0].shape[1:]
    return call(
        place_kernel,
        jax.ShapeDtypeStruct(shape, jnp.bfloat16),
        [pltpu.SemaphoreType.DMA((RING,))],
        "placed",
        [SMEM] + [ANY] * RING,
        ANY,
    )(mine, *pieces)


def local(tokens, w_tiles, tile_rows, tile_count, grad_hidden):
    panels, slots, tile = w_tiles.shape[1:4]
    shard, width = tokens.shape
    blocks = width // tile
    rows, count, w = tile_rows.reshape(-1), tile_count.reshape(-1), w_tiles[0]
    at = lax.axis_index("col")
    at_x, at_z = at // RING, at % RING
    row = lax.axis_index("row")
    mine = lax.axis_index("dp").astype(jnp.int32).reshape(1)

    seen = jnp.bitwise_xor((at_x + jnp.arange(RING)) % RING, row)
    slot_of_step = ((seen % 2) * 2 + seen // 2).astype(jnp.int32)

    gelu_fn = partial(jax.nn.gelu, approximate=True)
    hold = lax.optimization_barrier

    def into_rows(keep, send):
        half = keep.astype(jnp.float32) + send.astype(jnp.float32)
        height = half.shape[0] // 2
        return half[:height], half[height:].astype(jnp.bfloat16)

    def activate(members, ours, theirs):
        pre_act = ours + theirs.astype(jnp.float32)
        act, backward = jax.vjp(gelu_fn, pre_act)
        cotangent = [
            lax.dynamic_slice_in_dim(grad_hidden, (at_z + j) % RING * shard, shard) for j in members
        ]
        cotangent = jnp.concatenate(cotangent, axis=0).astype(jnp.float32)
        return act.astype(jnp.bfloat16), backward(cotangent)[0].astype(jnp.bfloat16)

    own = tokens
    x1, x3, x2 = along_x(own, -1), along_x(own, 1), along_x(own, 2)
    z1, z3 = along_z(own, -1), along_z(own, 1)
    down, across = live_tiles(count, w)
    z1, z3, x1, x3, x2, own, down, across = hold((z1, z3, x1, x3, x2, own, down, across))

    both = jnp.concatenate([z1, z3], axis=0)
    both1, both3 = along_x(both, -1), along_x(both, 1)
    z2 = along_z(own, 2)
    keep0, send0, xt0 = forward(
        rows, slot_of_step, ([own], [x1], [x2], [x3]), down, flops=1_000_000_000
    )
    both, both1, both3, z2, x2, keep0, send0, xt0 = hold(
        (both, both1, both3, z2, x2, keep0, send0, xt0)
    )

    z1x2, z3x2 = along_x(both3[:shard], 1), along_x(both1[shard:], -1)
    z2x1, z2x3 = along_x(z2, -1), along_x(z2, 1)
    ours0, theirs0 = into_rows(keep0, swap_core(send0))
    theirs0 = swap_chip(theirs0)
    z1x2, z3x2, z2x1, z2x3, theirs0 = hold((z1x2, z3x2, z2x1, z2x3, theirs0))
    z2x2 = along_x(z2, 2)
    keep1, send1, xt1 = forward(
        rows, slot_of_step, ([both], [both1], [z1x2, z3x2], [both3]), down
    )
    z2x2, send1, theirs0 = hold((z2x2, send1, theirs0))

    act0, grad0 = activate((0,), ours0, theirs0)
    ours1, theirs1 = into_rows(keep1, swap_core(send1))
    theirs1, grad0, z2x2 = hold((theirs1, grad0, z2x2))
    theirs1, other0 = swap_chip(theirs1), swap_chip(grad0)
    keep2, send2, xt2 = forward(rows, slot_of_step, ([z2], [z2x1], [z2x2], [z2x3]), down)
    theirs1, other0, keep2, send2 = hold((theirs1, other0, keep2, send2))
    ours2, theirs2 = into_rows(keep2, swap_core(send2))
    act1, grad1 = activate((1, 3), ours1, theirs1)
    grad1, theirs2 = hold((grad1, theirs2))

    other1, theirs2 = swap_chip(grad1), swap_chip(theirs2)
    grad1c = swap_core(grad1)
    slots0 = [grad0, other0, swap_core(grad0), swap_core(other0)]
    theirs2, grad1c, slots0 = hold((theirs2, grad1c, slots0))
    act2, grad2 = activate((2,), ours2, theirs2)
    grad2, slots0 = hold((grad2, slots0))
    other2, grad2c = swap_chip(grad2), swap_core(grad2)
    split = partial(input_grad, rows, count, slot_of_step, w=across, blocks=blocks)
    single = [(i, 0, shard) for i in range(RING)]
    double = [(0, 0, 2 * shard), (1, 0, 2 * shard), (2, 0, shard), (2, shard, shard), (3, 0, 2 * shard)]
    p0 = split(slots0, layout=single)
    other1, grad2c, p0 = hold((other1, grad2c, p0))
    near1, near3, near2 = along_x(p0[1], 1), along_x(p0[3], -1), along_x(p0[2], 2)
    slots1 = [grad1, other1, grad1c, swap_core(other1)]
    a0, a1, a2, a3, a4 = split(slots1, layout=double)
    slots2 = [grad2, other2, grad2c, swap_core(other2)]
    a2, a3, slots2 = hold((a2, a3, slots2))

    up, dn = along_x(a2, 1), along_x(a3, -1)
    weights = partial(
        weight_grad, rows, count, mine, pieces=slots0 + slots1 + slots2, slots=slots
    )
    q2, q2h = weights((xt0, xt1, xt2), steps=(2,), cut=2)
    q2, q2h, slots2, near1, near2, near3 = hold((q2, q2h, slots2, near1, near2, near3))
    q2, q2h = along_y(q2, 1), along_y(q2h, -1)
    p2 = split(slots2, layout=single)
    up, dn, p2, xt0, xt1, xt2 = hold((up, dn, p2, xt0, xt1, xt2))
    far1, far3, far2 = along_x(p2[1], 1), along_x(p2[3], -1), along_x(p2[2], 2)
    up = jnp.concatenate([add(a1[:shard], up), a1[shard:]], axis=0)
    dn = jnp.concatenate([a4[:shard], add(a4[shard:], dn)], axis=0)
    q1, q3 = weights((xt0, xt1, xt2), steps=(1, 3), flops=100_000_000)
    q1, q3, q2, q2h, up, dn, xt0, xt1, xt2 = hold((q1, q3, q2, q2h, up, dn, xt0, xt1, xt2))
    half = slots // 2
    q1 = jnp.concatenate([add(q1[:, :half], q2), q1[:, half:]], axis=1)
    q3 = jnp.concatenate([q3[:, :half], add(q3[:, half:], q2h)], axis=1)
    q1, q3, xt0, xt1, xt2 = hold((q1, q3, xt0, xt1, xt2))
    q1, q3 = along_y(q1, 1), along_y(q3, -1)
    (q0,) = weights((xt0, xt1, xt2), steps=(0,))
    near = add(p0[0], near1, near3, near2)
    hidden = jnp.zeros(grad_hidden.shape, jnp.bfloat16)
    for j, act in ((0, act0), (1, act1[:shard]), (3, act1[shard:]), (2, act2)):
        hidden = lax.dynamic_update_slice(hidden, act, ((at_z + j) % RING * shard, 0))
    up, dn = along_x(up, 1), along_x(dn, -1)
    far1, far3, far2, q0 = hold((far1, far3, far2, q0))
    far = along_z(add(p2[0], far1, far3, far2), 2)
    q1, q3, hidden, near = hold((q1, q3, hidden, near))

    quarter = add(q0, q1, q3)
    quarter, up, dn = hold((quarter, up, dn))
    ahead, behind = add(a0[:shard], up[:shard], dn[:shard]), add(a0[shard:], up[shard:], dn[shard:])
    ahead, behind = along_z(ahead, 1), along_z(behind, -1)
    q1, q3, q2 = along_y(quarter, -1), along_y(quarter, 1), along_y(quarter, 2)
    ahead, behind, far, q1, q3, q2 = hold((ahead, behind, far, q1, q3, q2))
    grad_x = add(near, far, ahead, behind)
    grad_w = placed(mine, [quarter, q1, q2, q3])
    return hidden, grad_x, grad_w[None]


def solution(mesh):
    return jax.shard_map(
        local,
        mesh=mesh,
        in_specs=(
            P(("dp", "col"), "row"),
            P("row", "col", None, None, None),
            P("row", "col", None),
            P("row", "col"),
            P(("dp", "row"), "col"),
        ),
        out_specs=(
            P(("dp", "row"), "col"),
            P(("dp", "col"), "row"),
            P("row", "col", None, None, None),
        ),
        check_vma=False,
    )
```

```python
from functools import partial

import jax
import jax.numpy as jnp
from jax import lax
from jax.experimental import pallas as pl
from jax.experimental.pallas import tpu as pltpu
from jax.sharding import PartitionSpec as P

VMEM_LIMIT = 24 * 1024 * 1024
RING = 4
COL = RING * RING
ROW = 4


def lanes(start, size):
    return pl.ds(pl.multiple_of(start * size, size), size)


def along_x(value, step):
    pairs = [(i, (i // RING + step) % RING * RING + i % RING) for i in range(COL)]
    return lax.ppermute(value, "col", pairs)


def along_z(value, step):
    pairs = [(i, i // RING * RING + (i % RING + step) % RING) for i in range(COL)]
    return lax.ppermute(value, "col", pairs)


def along_y(value, step):
    size = lax.axis_size("dp")
    return lax.ppermute(value, "dp", [(i, (i + step) % size) for i in range(size)])


def swap_core(value):
    return lax.ppermute(value, "row", [(i, i ^ 1) for i in range(ROW)])


def swap_chip(value):
    return lax.ppermute(value, "row", [(i, i ^ 2) for i in range(ROW)])


def add(*values):
    return sum(v.astype(jnp.float32) for v in values).astype(jnp.bfloat16)


ANY = pl.BlockSpec(memory_space=pl.ANY)
SMEM = pl.BlockSpec(memory_space=pltpu.SMEM)
VMEM = pl.BlockSpec(memory_space=pltpu.VMEM)


def run(copies):
    for copy in copies:
        copy.start()
    for copy in copies:
        copy.wait()


def call(kernel, out_shape, scratch, name, in_specs, out_specs, flops=20_000_000_000):
    return pl.pallas_call(
        kernel,
        in_specs=in_specs,
        out_specs=out_specs,
        out_shape=out_shape,
        scratch_shapes=scratch,
        compiler_params=pltpu.CompilerParams(vmem_limit_bytes=VMEM_LIMIT),
        cost_estimate=pl.CostEstimate(flops=flops, bytes_accessed=0, transcendentals=0),
        name=name,
    )


def live_kernel(count, w_ref, down_ref, across_ref):
    panels, slots, tile, _ = w_ref.shape

    def body(p, carry):
        for k in range(slots):
            block = w_ref[p, k] * (count[p] > k).astype(jnp.bfloat16)
            at = slice(k * tile, (k + 1) * tile)
            down_ref[p, at] = block
            across_ref[p, :, at] = block.T
        return carry

    lax.fori_loop(0, panels, body, 0)


def live_tiles(count, w):
    panels, slots, tile, _ = w.shape
    return call(
        live_kernel,
        [
            jax.ShapeDtypeStruct((panels, slots * tile, tile), jnp.bfloat16),
            jax.ShapeDtypeStruct((panels, tile, slots * tile), jnp.bfloat16),
        ],
        [],
        "live_tiles",
        [SMEM, VMEM],
        [VMEM] * 2,
    )(count, w)


def forward_kernel(layout, rows, place, *refs):
    number = len(layout)
    pieces, (w_ref, keep, send, xt_ref, x_ref, sems) = refs[:number], refs[number:]
    panels, depth, tile = w_ref.shape
    slots = depth // tile
    height = x_ref.shape[0] // RING
    run(
        [
            pltpu.make_async_copy(
                piece,
                x_ref.at[pl.ds(pl.multiple_of(place[i] * height + at, 64), piece.shape[0])],
                sems.at[n],
            )
            for n, (piece, (i, at)) in enumerate(zip(pieces, layout))
        ]
    )
    half = keep.shape[0]
    per_panel = xt_ref.shape[0] // panels

    def body(p, carry):
        weights = w_ref[p]
        for first in range(0, x_ref.shape[0], 256):
            at = slice(first, first + 256)
            chosen = [x_ref[at, lanes(rows[p * slots + k], tile)] for k in range(slots)]
            total = jnp.dot(
                jnp.concatenate(chosen, axis=1), weights, preferred_element_type=jnp.float32
            ).astype(jnp.bfloat16)
            for top in range(first, first + 256, 128):
                out = keep if top < half else send
                out[top % half : top % half + 128, lanes(p, tile)] = total[
                    top - first : top - first + 128
                ]
        for n in range(per_panel):
            block = p * per_panel + n
            xt_ref[block] = x_ref[:, lanes(block, tile)].T
        return carry

    lax.fori_loop(0, panels, body, 0)


def forward(rows, place, steps, w, **cost):
    pieces, layout = [], []
    for i, arrays in enumerate(steps):
        at = 0
        for array in arrays:
            pieces.append(array)
            layout.append((i, at))
            at += array.shape[0]
    tokens, width = RING * at, pieces[0].shape[1]
    panels, _, tile = w.shape
    blocks = width // tile
    half = jax.ShapeDtypeStruct((tokens // 2, panels * tile), jnp.bfloat16)
    return call(
        partial(forward_kernel, layout),
        [half, half, jax.ShapeDtypeStruct((blocks, tile, tokens), jnp.bfloat16)],
        [pltpu.VMEM((tokens, width), jnp.bfloat16), pltpu.SemaphoreType.DMA((len(pieces),))],
        "forward",
        [SMEM] * 2 + [ANY] * len(pieces) + [VMEM],
        [VMEM] * 3,
        **cost,
    )(rows, place, *pieces, w)


def input_kernel(layout, rows, count, place, g0, g1, g2, g3, w_ref, *refs):
    outs, (g_ref, sum_ref, sems) = refs[: len(layout)], refs[len(layout) :]
    panels, tile, depth = w_ref.shape
    slots = depth // tile
    height = g0.shape[0]
    run(
        [
            pltpu.make_async_copy(piece, g_ref.at[pl.ds(s * height, height)], sems.at[s])
            for s, piece in enumerate((g0, g1, g2, g3))
        ]
    )
    sum_ref[...] = jnp.zeros_like(sum_ref)
    half = slots // 2

    def body(p, carry):
        live = count[p]

        def spread(first):
            weights = w_ref[p, :, first * tile : (first + half) * tile]
            for top in range(0, g_ref.shape[0], 256):
                at = slice(top, top + 256)
                terms = jnp.dot(
                    g_ref[at, lanes(p, tile)], weights, preferred_element_type=jnp.float32
                )
                for k in range(half):
                    sum_ref[rows[p * slots + first + k], at] += terms[:, k * tile : (k + 1) * tile]

        spread(0)

        @pl.when(live > half)
        def _():
            spread(half)

        return carry

    lax.fori_loop(0, panels, body, 0)
    for out, (i, at) in zip(outs, layout):
        start = pl.multiple_of(place[i] * height + at, 64)
        for r in range(sum_ref.shape[0]):
            out[:, r * tile : (r + 1) * tile] = sum_ref[
                r, pl.ds(start, out.shape[0])
            ].astype(jnp.bfloat16)


def input_grad(rows, count, place, slot_grads, w, blocks, layout):
    panels, tile, _ = w.shape
    height = slot_grads[0].shape[0]
    tokens = RING * height
    outs = [jax.ShapeDtypeStruct((size, blocks * tile), jnp.bfloat16) for _, _, size in layout]
    return call(
        partial(input_kernel, [(i, at) for i, at, _ in layout]),
        outs,
        [
            pltpu.VMEM((tokens, panels * tile), jnp.bfloat16),
            pltpu.VMEM((blocks, tokens, tile), jnp.float32),
            pltpu.SemaphoreType.DMA((RING,)),
        ],
        "input_grad",
        [SMEM] * 3 + [ANY] * RING + [VMEM],
        [VMEM] * len(outs),
    )(rows, count, place, *slot_grads, w)


def weight_kernel(parts, steps, rows, count, mine, *refs):
    xts, pieces = refs[:parts], refs[parts : parts + RING * parts]
    outs, (g_ref, sum_ref, sems) = refs[parts + RING * parts : -3], refs[-3:]
    _, per_step, slots, tile, _ = sum_ref.shape
    half = slots // 2
    copies, width = [], per_step * tile
    for step in steps:
        at = 0
        used = pl.ds(pl.multiple_of(lax.rem(mine[0] + step, RING) * width, width), width)
        for piece in pieces:
            copies.append(
                pltpu.make_async_copy(
                    piece.at[:, used],
                    g_ref.at[pl.ds(at, piece.shape[0]), used],
                    sems.at[len(copies)],
                )
            )
            at += piece.shape[0]
    run(copies)

    def body(out, step, inner, carry):
        panel = lax.rem(mine[0] + step, RING) * per_step + inner
        live = count[panel]

        def product(first):
            total = jnp.zeros((half * tile, tile), jnp.float32)
            at = 0
            for xt in xts:
                chosen = [xt[rows[panel * slots + first + k]] for k in range(half)]
                total += jnp.dot(
                    jnp.concatenate(chosen, axis=0),
                    g_ref[at : at + xt.shape[2], lanes(panel, tile)],
                    preferred_element_type=jnp.float32,
                )
                at += xt.shape[2]
            for k in range(half):
                block = total[k * tile : (k + 1) * tile]
                sum_ref[out, inner, first + k] = jnp.where(
                    live > first + k, block, 0.0
                ).astype(jnp.bfloat16)

        product(0)

        @pl.when(live > half)
        def _():
            product(half)

        @pl.when(live <= half)
        def _():
            sum_ref[out, inner, half:] = jnp.zeros((slots - half, tile, tile), jnp.bfloat16)

        return carry

    copies, done = [], 0
    for i, step in enumerate(steps):
        lax.fori_loop(0, per_step, partial(body, i, step), 0)
        at = 0
        while at < slots:
            out = outs[done]
            copies.append(
                pltpu.make_async_copy(
                    sum_ref.at[i, :, pl.ds(at, out.shape[1])], out, sems.at[done]
                )
            )
            copies[-1].start()
            at, done = at + out.shape[1], done + 1
    for copy in copies:
        copy.wait()


def weight_grad(rows, count, mine, xts, pieces, slots, steps, cut=1, **cost):
    blocks, tile, _ = xts[0].shape
    panels = pieces[0].shape[1] // tile
    tokens = sum(piece.shape[0] for piece in pieces)
    quarter = (panels // RING, slots, tile, tile)
    return call(
        partial(weight_kernel, len(xts), steps),
        [jax.ShapeDtypeStruct((panels // RING, slots // cut, tile, tile), jnp.bfloat16)]
        * (cut * len(steps)),
        [
            pltpu.VMEM((tokens, panels * tile), jnp.bfloat16),
            pltpu.VMEM((len(steps),) + quarter, jnp.bfloat16),
            pltpu.SemaphoreType.DMA((len(pieces) * len(steps),)),
        ],
        "weight_grad",
        [SMEM] * 3 + [VMEM] * len(xts) + [ANY] * len(pieces),
        [ANY] * (cut * len(steps)),
        **cost,
    )(rows, count, mine, *xts, *pieces)


def place_kernel(mine, p0, p1, p2, p3, out, sems):
    size = p0.shape[0]
    run(
        [
            pltpu.make_async_copy(
                piece, out.at[pl.ds(lax.rem(mine[0] + i, RING) * size, size)], sems.at[i]
            )
            for i, piece in enumerate((p0, p1, p2, p3))
        ]
    )


def placed(mine, pieces):
    shape = (RING * pieces[0].shape[0],) + pieces[0].shape[1:]
    return call(
        place_kernel,
        jax.ShapeDtypeStruct(shape, jnp.bfloat16),
        [pltpu.SemaphoreType.DMA((RING,))],
        "placed",
        [SMEM] + [ANY] * RING,
        ANY,
    )(mine, *pieces)


def local(tokens, w_tiles, tile_rows, tile_count, grad_hidden):
    panels, slots, tile = w_tiles.shape[1:4]
    shard, width = tokens.shape
    blocks = width // tile
    rows, count, w = tile_rows.reshape(-1), tile_count.reshape(-1), w_tiles[0]
    at = lax.axis_index("col")
    at_x, at_z = at // RING, at % RING
    row = lax.axis_index("row")
    mine = lax.axis_index("dp").astype(jnp.int32).reshape(1)

    seen = jnp.bitwise_xor((at_x + jnp.arange(RING)) % RING, row)
    slot_of_step = ((seen % 2) * 2 + seen // 2).astype(jnp.int32)

    gelu_fn = partial(jax.nn.gelu, approximate=True)
    hold = lax.optimization_barrier

    def into_rows(keep, send):
        half = keep.astype(jnp.float32) + send.astype(jnp.float32)
        height = half.shape[0] // 2
        return half[:height], half[height:].astype(jnp.bfloat16)

    def activate(members, ours, theirs):
        pre_act = ours + theirs.astype(jnp.float32)
        act, backward = jax.vjp(gelu_fn, pre_act)
        cotangent = [
            lax.dynamic_slice_in_dim(grad_hidden, (at_z + j) % RING * shard, shard) for j in members
        ]
        cotangent = jnp.concatenate(cotangent, axis=0).astype(jnp.float32)
        return act.astype(jnp.bfloat16), backward(cotangent)[0].astype(jnp.bfloat16)

    own = tokens
    x1, x3, x2 = along_x(own, -1), along_x(own, 1), along_x(own, 2)
    z1, z3 = along_z(own, -1), along_z(own, 1)
    down, across = live_tiles(count, w)
    z1, z3, x1, x3, x2, own, down, across = hold((z1, z3, x1, x3, x2, own, down, across))

    both = jnp.concatenate([z1, z3], axis=0)
    both1, both3 = along_x(both, -1), along_x(both, 1)
    z2 = along_z(own, 2)
    keep0, send0, xt0 = forward(
        rows, slot_of_step, ([own], [x1], [x2], [x3]), down, flops=1_000_000_000
    )
    both, both1, both3, z2, x2, keep0, send0, xt0 = hold(
        (both, both1, both3, z2, x2, keep0, send0, xt0)
    )

    z1x2, z3x2 = along_x(both3[:shard], 1), along_x(both1[shard:], -1)
    z2x1, z2x3 = along_x(z2, -1), along_x(z2, 1)
    ours0, theirs0 = into_rows(keep0, swap_core(send0))
    theirs0 = swap_chip(theirs0)
    z1x2, z3x2, z2x1, z2x3, theirs0 = hold((z1x2, z3x2, z2x1, z2x3, theirs0))
    z2x2 = along_x(z2, 2)
    keep1, send1, xt1 = forward(
        rows, slot_of_step, ([both], [both1], [z1x2, z3x2], [both3]), down
    )
    z2x2, send1, theirs0 = hold((z2x2, send1, theirs0))

    act0, grad0 = activate((0,), ours0, theirs0)
    ours1, theirs1 = into_rows(keep1, swap_core(send1))
    theirs1, grad0, z2x2 = hold((theirs1, grad0, z2x2))
    theirs1, other0 = swap_chip(theirs1), swap_chip(grad0)
    keep2, send2, xt2 = forward(rows, slot_of_step, ([z2], [z2x1], [z2x2], [z2x3]), down)
    theirs1, other0, keep2, send2 = hold((theirs1, other0, keep2, send2))
    ours2, theirs2 = into_rows(keep2, swap_core(send2))
    act1, grad1 = activate((1, 3), ours1, theirs1)
    grad1, theirs2 = hold((grad1, theirs2))

    other1, theirs2 = swap_chip(grad1), swap_chip(theirs2)
    grad1c = swap_core(grad1)
    slots0 = [grad0, other0, swap_core(grad0), swap_core(other0)]
    theirs2, grad1c, slots0 = hold((theirs2, grad1c, slots0))
    act2, grad2 = activate((2,), ours2, theirs2)
    grad2, slots0 = hold((grad2, slots0))
    other2, grad2c = swap_chip(grad2), swap_core(grad2)
    split = partial(input_grad, rows, count, slot_of_step, w=across, blocks=blocks)
    single = [(i, 0, shard) for i in range(RING)]
    double = [(0, 0, 2 * shard), (1, 0, 2 * shard), (2, 0, shard), (2, shard, shard), (3, 0, 2 * shard)]
    p0 = split(slots0, layout=single)
    other1, grad2c, p0 = hold((other1, grad2c, p0))
    near1, near3, near2 = along_x(p0[1], 1), along_x(p0[3], -1), along_x(p0[2], 2)
    slots1 = [grad1, other1, grad1c, swap_core(other1)]
    a0, a1, a2, a3, a4 = split(slots1, layout=double)
    slots2 = [grad2, other2, grad2c, swap_core(other2)]
    a2, a3, slots2 = hold((a2, a3, slots2))

    up, dn = along_x(a2, 1), along_x(a3, -1)
    weights = partial(
        weight_grad, rows, count, mine, pieces=slots0 + slots1 + slots2, slots=slots
    )
    q2, q2h = weights((xt0, xt1, xt2), steps=(2,), cut=2)
    q2, q2h, slots2, near1, near2, near3 = hold((q2, q2h, slots2, near1, near2, near3))
    q2, q2h = along_y(q2, 1), along_y(q2h, -1)
    p2 = split(slots2, layout=single)
    up, dn, p2, xt0, xt1, xt2 = hold((up, dn, p2, xt0, xt1, xt2))
    far1, far3, far2 = along_x(p2[1], 1), along_x(p2[3], -1), along_x(p2[2], 2)
    up = jnp.concatenate([add(a1[:shard], up), a1[shard:]], axis=0)
    dn = jnp.concatenate([a4[:shard], add(a4[shard:], dn)], axis=0)
    q1, q3 = weights((xt0, xt1, xt2), steps=(1, 3), flops=100_000_000)
    q1, q3, q2, q2h, up, dn, xt0, xt1, xt2 = hold((q1, q3, q2, q2h, up, dn, xt0, xt1, xt2))
    half = slots // 2
    q1 = jnp.concatenate([add(q1[:, :half], q2), q1[:, half:]], axis=1)
    q3 = jnp.concatenate([q3[:, :half], add(q3[:, half:], q2h)], axis=1)
    q1, q3, xt0, xt1, xt2 = hold((q1, q3, xt0, xt1, xt2))
    q1, q3 = along_y(q1, 1), along_y(q3, -1)
    (q0,) = weights((xt0, xt1, xt2), steps=(0,))
    near = add(p0[0], near1, near3, near2)
    hidden = jnp.zeros(grad_hidden.shape, jnp.bfloat16)
    for j, act in ((0, act0), (1, act1[:shard]), (3, act1[shard:]), (2, act2)):
        hidden = lax.dynamic_update_slice(hidden, act, ((at_z + j) % RING * shard, 0))
    up, dn = along_x(up, 1), along_x(dn, -1)
    far1, far3, far2, q0 = hold((far1, far3, far2, q0))
    far = along_z(add(p2[0], far1, far3, far2), 2)
    q1, q3, hidden, near = hold((q1, q3, hidden, near))

    quarter = add(q0, q1, q3)
    q1, q3 = along_y(quarter, -1), along_y(quarter, 1)
    quarter, up, dn = hold((quarter, up, dn))
    ahead, behind = add(a0[:shard], up[:shard], dn[:shard]), add(a0[shard:], up[shard:], dn[shard:])
    q2 = along_y(quarter, 2)
    ahead, behind = along_z(ahead, 1), along_z(behind, -1)
    q1, q3, far = hold((q1, q3, far))
    ahead, behind, far, q2 = hold((ahead, behind, far, q2))
    grad_x = add(near, far, ahead, behind)
    grad_w = placed(mine, [quarter, q1, q2, q3])
    return hidden, grad_x, grad_w[None]


def solution(mesh):
    return jax.shard_map(
        local,
        mesh=mesh,
        in_specs=(
            P(("dp", "col"), "row"),
            P("row", "col", None, None, None),
            P("row", "col", None),
            P("row", "col"),
            P(("dp", "row"), "col"),
        ),
        out_specs=(
            P(("dp", "row"), "col"),
            P(("dp", "col"), "row"),
            P("row", "col", None, None, None),
        ),
        check_vma=False,
    )
```
